256 devices in a mesh: dp: 32 (over z, y), tensor: 8 (over x, core).
Axes of the slice: x: 4, y: 4, z: 8, core: 2. Of those that a mesh axis runs over, the one named last changes fastest.
Arguments:
- queries: bfloat16 [96, 256, 8192], P('dp', None, 'tensor'), may hold values from -6 to 6
- response_keys: bfloat16 [96, 256, 1024], P('dp', None, 'tensor'), may hold values from -6 to 6
- response_values: bfloat16 [96, 256, 1024], P('dp', None, 'tensor'), may hold values from -6 to 6
- out_grad: bfloat16 [96, 256, 5120], P('dp', 'tensor'), may hold values from -6 to 6
- advantages: float32 [96, 256], P('dp', 'tensor'), may hold values from -4 to 4
- lengths: int32 [96], P('dp'), may hold values from 128 to 256, as said below
- groups: int32 [96], P('dp'), may hold values from 0 to 31, as said below
- prompt_keys: bfloat16 [32, 256, 1024], P('dp', None, 'tensor'), may hold values from -6 to 6
- prompt_value_rows: bfloat16 [32, 256, 1024], P('dp', None, 'tensor'), may hold values from -6 to 6
- w_out: bfloat16 [5120, 8192], P('dp', 'tensor'), may hold values from -0.078125 to 0.078125
Outputs:
- query_grad: bfloat16 [96, 256, 8192], P('dp', None, 'tensor')
- key_grad: bfloat16 [96, 256, 1024], P('dp', None, 'tensor')
- value_grad: bfloat16 [96, 256, 1024], P('dp', None, 'tensor')
- prompt_key_grad: float32 [32, 256, 1024], P('dp', None, 'tensor')
- prompt_value_grad: float32 [32, 256, 1024], P('dp', None, 'tensor')
The draws below stay inside these ranges and needn't reach their ends.
Inputs may be any that keep to these rules, and one draw needn't show every extreme that they name: lengths are multiples of 128; some response has 256. groups[s] = (s // 3 + o) mod 32 with o between -2 and 2; both ends of o occur in every draw; the number of responses of a prompt varies.
All inputs are finite; a program needn't handle non-finite values.
Results may differ from the reference program's by a relative error of at most 0.0086.
Values may be sent and summed in bfloat16 or wider, within the bound.
No kernel may reach another device: no remote copies, remote signals or barrier semaphores. Data moves between devices by JAX's collectives and lax.ppermute only.
A program may use at most 128 MiB of HBM per device.

```python
import jax
import jax.numpy as jnp
from jax import lax

D = 5120
HQ = 64
KEY_VALUE_HEADS = 8
HEAD_SIZE = 128
R_DEV = 3
RESPONSE_LENGTH = 256
PROMPT_LENGTH = 256
LGRAN = 128
SPREAD = 2
RESPONSE_COUNT = 96
PROMPT_COUNT = 32


def draw_queries(key, part):
    key = jax.random.fold_in(key, 5)
    key_one = jax.random.fold_in(key, 0)
    sampled_values = jnp.clip(jax.random.normal(key_one, (RESPONSE_COUNT, RESPONSE_LENGTH, HQ * HEAD_SIZE), jnp.float32), -6.0, 6.0)
    return sampled_values.astype(jnp.bfloat16)


def draw_prompt_keys(key, part):
    key = jax.random.fold_in(key, 6)
    sampled_values = jnp.clip(jax.random.normal(key, (PROMPT_COUNT, PROMPT_LENGTH, KEY_VALUE_HEADS * HEAD_SIZE), jnp.float32), -6.0, 6.0)
    return sampled_values.astype(jnp.bfloat16)


def draw_lengths(key, part):
    key = jax.random.fold_in(key, 7)
    key_one, key_two = jax.random.split(key)
    length_units = jax.random.randint(key_one, (RESPONSE_COUNT,), 1, RESPONSE_LENGTH // LGRAN + 1)
    forced = jax.random.randint(key_two, (), 0, RESPONSE_COUNT)
    length_units = jnp.where(jnp.arange(RESPONSE_COUNT) == forced, RESPONSE_LENGTH // LGRAN, length_units)
    return (length_units * LGRAN).astype(jnp.int32)


def draw_groups(key, part):
    key = jax.random.fold_in(key, 11)
    key_one, key_two, key_three = jax.random.split(key, 3)
    owners = jnp.arange(RESPONSE_COUNT, dtype=jnp.int32) // R_DEV
    offsets = jax.random.randint(key_one, (RESPONSE_COUNT,), -SPREAD, SPREAD + 1)
    low_slot = jax.random.randint(key_two, (), 0, RESPONSE_COUNT)
    high_slot = (low_slot + 1 + jax.random.randint(key_three, (), 0, RESPONSE_COUNT - 1)) % RESPONSE_COUNT
    slot_ids = jnp.arange(RESPONSE_COUNT)
    offsets = jnp.where(slot_ids == low_slot, -SPREAD, offsets)
    offsets = jnp.where(slot_ids == high_slot, SPREAD, offsets)
    return ((owners + offsets) % PROMPT_COUNT).astype(jnp.int32)


def level_of(stream_key, shape, pieces, low, largest):
    gain = 1.0
    for position, shards_of in pieces:
        heights = jax.random.uniform(jax.random.fold_in(jax.random.fold_in(stream_key, 6), position), (shards_of,), jnp.float32, low / len(pieces), largest / len(pieces))
        gain = gain * jnp.repeat(jnp.exp(heights), shape[position] // shards_of).reshape((-1,) + (1,) * (len(shape) - 1 - position))
    return gain


def noise(key, extent, scale, reach, cuts=(), kind=jnp.bfloat16):
    factor_of = level_of(key, extent, cuts, -0.22, 0.18) if cuts else 1.0
    array = jax.random.normal(key, extent, jnp.float32) * scale * factor_of
    return jnp.minimum(jnp.maximum(array, -reach), reach).astype(kind)


def setup_inputs(seed: int = 0) -> dict:
    streams_of = jax.random.split(jax.random.key(seed), 11)
    return {
        "queries": draw_queries(jax.random.fold_in(streams_of[10], 71), 0),
        "response_keys": noise(streams_of[1], (RESPONSE_COUNT, RESPONSE_LENGTH, KEY_VALUE_HEADS * HEAD_SIZE), 1.0, 6.0, ((0, 32), (2, 8))),
        "response_values": noise(streams_of[2], (RESPONSE_COUNT, RESPONSE_LENGTH, KEY_VALUE_HEADS * HEAD_SIZE), 1.0, 6.0, ((0, 32), (2, 8))),
        "out_grad": noise(streams_of[3], (RESPONSE_COUNT, RESPONSE_LENGTH, D), 1.0, 6.0, ((0, 32), (1, 8))),
        "advantages": noise(streams_of[4], (RESPONSE_COUNT, RESPONSE_LENGTH), 1.0, 4.0, ((0, 32), (1, 8)), jnp.float32),
        "lengths": draw_lengths(jax.random.fold_in(streams_of[10], 71), 0),
        "groups": draw_groups(jax.random.fold_in(streams_of[10], 71), 0),
        "prompt_keys": draw_prompt_keys(jax.random.fold_in(streams_of[10], 71), 0),
        "prompt_value_rows": noise(streams_of[8], (PROMPT_COUNT, PROMPT_LENGTH, KEY_VALUE_HEADS * HEAD_SIZE), 1.0, 6.0, ((0, 32), (2, 8))),
        "w_out": noise(streams_of[9], (D, HQ * HEAD_SIZE), D ** -0.5, 0.078125, ((0, 32), (1, 8))),
    }


loss_scale = 16.0
mask_value = -1.0e30


def lowered(values):
    return lax.optimization_barrier(values.astype(jnp.bfloat16)).astype(jnp.float32)


def attend(query_rows, key_rows, value_rows, grad_rows, prompt_len):
    query_len = query_rows.shape[0]
    key_len = key_rows.shape[0]
    kv_heads = key_rows.shape[1] // HEAD_SIZE
    group = query_rows.shape[1] // HEAD_SIZE // kv_heads
    head_scale = HEAD_SIZE ** -0.5
    query_heads = query_rows.astype(jnp.float32).reshape(query_len, kv_heads, group, HEAD_SIZE)
    key_heads = key_rows.astype(jnp.float32).reshape(key_len, kv_heads, HEAD_SIZE)
    value_heads = value_rows.astype(jnp.float32).reshape(key_len, kv_heads, HEAD_SIZE)
    grad_heads = grad_rows.astype(jnp.float32).reshape(query_len, kv_heads, group, HEAD_SIZE)
    scores = jnp.einsum("qkgd,lkd->kgql", query_heads, key_heads) * head_scale
    query_pos = jnp.arange(query_len, dtype=jnp.int32)[:, None]
    key_pos = jnp.arange(key_len, dtype=jnp.int32)[None, :]
    allowed = (key_pos < prompt_len) | (key_pos - prompt_len <= query_pos)
    scores = jnp.where(allowed, scores, mask_value)
    weights = jax.nn.softmax(scores, axis=-1)
    weights_low = lowered(weights)
    dweights = jnp.einsum("qkgd,lkd->kgql", grad_heads, value_heads)
    dscores = weights * (dweights - jnp.sum(weights * dweights, axis=-1, keepdims=True))
    dscores_low = lowered(dscores)
    query_grad = jnp.einsum("kgql,lkd->qkgd", dscores_low, key_heads) * head_scale
    key_grad = jnp.einsum("kgql,qkgd->lkd", dscores_low, query_heads) * head_scale
    value_grad = jnp.einsum("kgql,qkgd->lkd", weights_low, grad_heads)
    return (query_grad.reshape(query_len, -1).astype(jnp.bfloat16),
            key_grad.reshape(key_len, -1), value_grad.reshape(key_len, -1))


def reference(queries, response_keys, response_values, out_grad, advantages, lengths, groups, prompt_keys, prompt_value_rows, w_out):
    positions = jnp.arange(RESPONSE_LENGTH, dtype=jnp.int32)

    def per_response(resp):
        live_len = lengths[resp]
        live_mask = jnp.where(positions < live_len, 1.0, 0.0).astype(jnp.float32)
        factor = advantages[resp] * live_mask * (loss_scale * RESPONSE_LENGTH / live_len.astype(jnp.float32))
        scaled = (out_grad[resp].astype(jnp.float32) * factor[:, None]).astype(jnp.bfloat16)
        d_out = jnp.dot(scaled, w_out, preferred_element_type=jnp.float32).astype(jnp.bfloat16)
        prompt_index = groups[resp].astype(jnp.int32)
        prompt_key_tile = lax.dynamic_index_in_dim(prompt_keys, prompt_index, 0, keepdims=False)
        prompt_value_tile = lax.dynamic_index_in_dim(prompt_value_rows, prompt_index, 0, keepdims=False)
        key_rows = jnp.concatenate([prompt_key_tile, response_keys[resp]], 0)
        value_rows = jnp.concatenate([prompt_value_tile, response_values[resp]], 0)
        query_grad, all_key, all_value = attend(queries[resp], key_rows, value_rows, d_out, PROMPT_LENGTH)
        return (query_grad, all_key[PROMPT_LENGTH:].astype(jnp.bfloat16), all_value[PROMPT_LENGTH:].astype(jnp.bfloat16),
                all_key[:PROMPT_LENGTH], all_value[:PROMPT_LENGTH])

    query_grad, key_grad, value_grad, prompt_key_part, prompt_value_part = lax.map(
        per_response, jnp.arange(RESPONSE_COUNT, dtype=jnp.int32))
    prompt_key_grad = jax.ops.segment_sum(prompt_key_part, groups, num_segments=PROMPT_COUNT)
    prompt_value_grad = jax.ops.segment_sum(prompt_value_part, groups, num_segments=PROMPT_COUNT)
    return query_grad, key_grad, value_grad, prompt_key_grad, prompt_value_grad
```

```python
import functools

import jax
import jax.numpy as jnp
from jax import lax
from jax.experimental import pallas as pl
from jax.experimental.pallas import tpu as pltpu
from jax.sharding import Mesh
from jax.sharding import PartitionSpec as P

HEAD_SIZE = 128
RESPONSE_LENGTH = 256
SPREAD = 2
Y_SIZE = 4
CORES = 2
VMEM_LIMIT = 60 * 2**20

loss_scale = 16.0
mask_value = -1e30
head_scale = HEAD_SIZE ** (-0.5)
F32 = jnp.float32
BF16 = jnp.bfloat16


def shift(block, axis, distance):
    count = lax.axis_size(axis)
    route = [(i, (i + distance) % count) for i in range(count)]
    return lax.ppermute(block, axis, route)


def ring_gather(block, axis, between=None):
    count = lax.axis_size(axis)
    rows = block.shape[0]
    pieces = [(0, 0, block)]
    up = down = block
    for step in range(1, count // 2):
        up = shift(up, axis, 1)
        down = shift(down, axis, -1)
        if between is not None:
            up, down = between(step, pieces, up, down)
        pieces += [(-step, 0, up), (step, 0, down)]
    far = count // 2
    half = rows // 2
    up, down = lax.optimization_barrier((up[:half], down[half:]))
    pieces += [(far, 0, shift(up, axis, 1)), (far, half, shift(down, axis, -1))]
    return pieces


def probs_kernel(q_ref, k_ref, out_ref, *, heads, prompt_len):
    keys = k_ref[0]
    own_len = keys.shape[0] - prompt_len
    query_len = q_ref.shape[1]
    row = lax.broadcasted_iota(jnp.int32, (own_len, query_len), 0)
    col = lax.broadcasted_iota(jnp.int32, (own_len, query_len), 1)
    for h in range(heads):
        q = q_ref[0, :, h * HEAD_SIZE:(h + 1) * HEAD_SIZE]
        scores = lax.dot_general(keys, q, (((1,), (1,)), ((), ())), preferred_element_type=F32) * head_scale
        top = scores[:prompt_len]
        low = jnp.where(row <= col, scores[prompt_len:], mask_value)
        peak = jnp.maximum(jnp.max(top, axis=0, keepdims=True), jnp.max(low, axis=0, keepdims=True))
        top = jnp.exp(top - peak)
        low = jnp.exp(low - peak)
        total = jnp.sum(top, axis=0, keepdims=True) + jnp.sum(low, axis=0, keepdims=True)
        inv = 1.0 / total
        cols = slice(h * query_len, (h + 1) * query_len)
        out_ref[0, :prompt_len, cols] = (top * inv).astype(BF16)
        out_ref[0, prompt_len:, cols] = (low * inv).astype(BF16)


def probs_of(queries, keys, prompt_len):
    slots, query_len, width = queries.shape
    key_len = keys.shape[1]
    heads = width // HEAD_SIZE
    return pl.pallas_call(
        functools.partial(probs_kernel, heads=heads, prompt_len=prompt_len),
        grid=(slots,),
        in_specs=[
            pl.BlockSpec((1, query_len, width), lambda r: (r, 0, 0)),
            pl.BlockSpec((1, key_len, HEAD_SIZE), lambda r: (r, 0, 0)),
        ],
        out_specs=pl.BlockSpec((1, key_len, heads * query_len), lambda r: (r, 0, 0)),
        out_shape=jax.ShapeDtypeStruct((slots, key_len, heads * query_len), BF16),
        compiler_params=pltpu.CompilerParams(vmem_limit_bytes=VMEM_LIMIT),
        cost_estimate=pl.CostEstimate(
            flops=4 * slots * heads * query_len * key_len * HEAD_SIZE,
            bytes_accessed=2 * slots * heads * query_len * key_len,
            transcendentals=slots * heads * query_len * key_len,
        ),
    )(queries, keys)


def blocks_of_a(a_pieces, order, shard_rows):
    out = []
    for at, dz in enumerate(order):
        parts = []
        for i, (dy, first, arr) in enumerate(a_pieces):
            source = at * shard_rows - first
            if 0 <= source < arr.shape[0]:
                parts.append((i, source, shard_rows, dy, 0))
        out.append((dz, tuple(parts)))
    return tuple(out)


def blocks_of_b(b_pieces, inner, shard_rows):
    out = {}
    for i, (dz, first, arr) in enumerate(b_pieces):
        parts = out.setdefault(dz, [])
        for k, dy in enumerate(inner):
            low, high = max(k * shard_rows, first), min((k + 1) * shard_rows, first + arr.shape[0])
            if low < high:
                parts.append((i, low - first, high - low, dy, low - k * shard_rows))
    return tuple((dz, tuple(parts)) for dz, parts in out.items())


def begin_loads(meta_ref, w_refs, scaled_ref, w_buf, scaled_buf, w_sems, s_sems, *, blocks, per_step, shard_rows, z_size):
    my_z, my_y = meta_ref[0], meta_ref[1]
    depth_z = Y_SIZE * shard_rows
    for at, (dz, parts) in enumerate(blocks):
        step, inside = at // per_step, at % per_step
        z = lax.rem(my_z + (dz + z_size), z_size)
        pltpu.make_async_copy(
            scaled_ref.at[:, :, pl.ds(pl.multiple_of(z * depth_z, HEAD_SIZE), depth_z)],
            scaled_buf.at[step, :, :, pl.ds(inside * depth_z, depth_z)],
            s_sems.at[step]).start()
        for i, source, rows, dy, first in parts:
            row = lax.rem(my_y + (dy + Y_SIZE), Y_SIZE) * shard_rows + (inside * depth_z + first)
            pltpu.make_async_copy(
                w_refs[i].at[pl.ds(source, rows), :],
                w_buf.at[step, pl.ds(pl.multiple_of(row, 16), rows), :], w_sems.at[step]).start()


def accumulate(acc, w_buf, scaled_buf, w_sems, s_sems):
    steps, slots, query_len, depth = scaled_buf.shape

    def multiply(step, carry):
        pltpu.make_async_copy(scaled_buf.at[step], scaled_buf.at[step], s_sems.at[step]).wait()
        pltpu.make_async_copy(w_buf.at[step], w_buf.at[step], w_sems.at[step]).wait()
        part = jnp.dot(scaled_buf[step].reshape(slots * query_len, depth), w_buf[step], preferred_element_type=F32)
        acc[...] += part.reshape(acc.shape)
        return carry

    lax.fori_loop(0, steps, multiply, 0)


def load_scratch(slots, query_len, cols, n_blocks, per_step, depth_z):
    steps = n_blocks // per_step
    return [
        pltpu.VMEM((steps, per_step * depth_z, cols), BF16),
        pltpu.VMEM((steps, slots, query_len, per_step * depth_z), BF16),
        pltpu.VMEM((slots, query_len, cols), F32),
        pltpu.SemaphoreType.DMA((steps,)),
        pltpu.SemaphoreType.DMA((steps,)),
    ]


def project_kernel(meta_ref, *refs, n_pieces, **loads):
    w_refs, (scaled_ref, out_ref, w_buf, scaled_buf, acc, w_sems, s_sems) = refs[:n_pieces], refs[n_pieces:]
    begin_loads(meta_ref, w_refs, scaled_ref, w_buf, scaled_buf, w_sems, s_sems, **loads)
    acc[...] = jnp.zeros_like(acc)
    accumulate(acc, w_buf, scaled_buf, w_sems, s_sems)
    out_ref[...] = acc[...].astype(out_ref.dtype)


def project(meta, pieces, blocks, per_step, scaled, dtype, shard_rows, z_size):
    slots, query_len, _ = scaled.shape
    cols = pieces[0].shape[1]
    depth_z = Y_SIZE * shard_rows
    anywhere = pl.BlockSpec(memory_space=pl.ANY)
    return pl.pallas_call(
        functools.partial(project_kernel, n_pieces=len(pieces), blocks=blocks, per_step=per_step,
                          shard_rows=shard_rows, z_size=z_size),
        grid_spec=pltpu.PrefetchScalarGridSpec(
            num_scalar_prefetch=1,
            grid=(1,),
            in_specs=[anywhere] * (len(pieces) + 1),
            out_specs=pl.BlockSpec((slots, query_len, cols), lambda i, m: (0, 0, 0)),
            scratch_shapes=load_scratch(slots, query_len, cols, len(blocks), per_step, depth_z),
        ),
        out_shape=jax.ShapeDtypeStruct((slots, query_len, cols), dtype),
        compiler_params=pltpu.CompilerParams(vmem_limit_bytes=VMEM_LIMIT),
        cost_estimate=pl.CostEstimate(
            flops=2 * slots * query_len * cols * depth_z * len(blocks),
            bytes_accessed=2 * depth_z * len(blocks) * (cols + slots * query_len),
            transcendentals=0,
        ),
    )(meta, *pieces, scaled)


def backward_kernel(meta_ref, *refs, n_pieces, heads, prompt_len, **loads):
    w_refs, refs = refs[:n_pieces], refs[n_pieces:]
    scaled_ref, probs_ref, part_ref, d_a_ref, q_ref, k_ref, v_ref, dq_ref, dk_ref, dv_ref, own_ref, *refs = refs
    sent_refs, refs = refs[:2 * SPREAD], refs[2 * SPREAD:]
    w_buf, scaled_buf, acc, w_sems, s_sems, probs_buf, do_buf, q_buf, ds_buf, sum_buf, p_sems = refs
    r = pl.program_id(0)
    slots, query_len = scaled_ref.shape[0], q_ref.shape[1]
    first_cols = d_a_ref.shape[2]

    @pl.when(r == 0)
    def _():
        begin_loads(meta_ref, w_refs, scaled_ref, w_buf, scaled_buf, w_sems, s_sems, **loads)
        for slot in range(slots):
            pltpu.make_async_copy(probs_ref.at[slot], probs_buf.at[slot], p_sems.at[slot]).start()
        sum_buf[...] = jnp.zeros_like(sum_buf)
        acc[...] = part_ref[...]
        accumulate(acc, w_buf, scaled_buf, w_sems, s_sems)

    pltpu.make_async_copy(probs_ref.at[r], probs_buf.at[r], p_sems.at[r]).wait()
    keys = k_ref[0]
    values = v_ref[0]
    for h in range(heads):
        rows = slice(h * query_len, (h + 1) * query_len)
        low, high = h * HEAD_SIZE, (h + 1) * HEAD_SIZE
        q_buf[rows, :] = q_ref[0, :, low:high]
        if high <= first_cols:
            d_out = d_a_ref[0, :, low:high]
        else:
            d_out = acc[r, :, low - first_cols:high - first_cols].astype(BF16)
        do_buf[rows, :] = d_out
        dprobs = lax.dot_general(values, d_out, (((1,), (1,)), ((), ())), preferred_element_type=F32)
        probs = probs_buf[r, :, rows].astype(F32)
        mean = jnp.sum(probs * dprobs, axis=0, keepdims=True)
        ds = (probs * (dprobs - mean)).astype(BF16)
        ds_buf[:, rows] = ds
        dq = lax.dot_general(ds, keys, (((0,), (0,)), ((), ())), preferred_element_type=F32) * head_scale
        dq_ref[0, :, low:high] = dq.astype(BF16)
    dk = jnp.dot(ds_buf[...], q_buf[...], preferred_element_type=F32) * head_scale
    dv = jnp.dot(probs_buf[r], do_buf[...], preferred_element_type=F32)
    dk_ref[0] = dk[prompt_len:].astype(BF16)
    dv_ref[0] = dv[prompt_len:].astype(BF16)
    offset = meta_ref[2 + r]
    for o in range(-SPREAD, SPREAD + 1):
        @pl.when(offset == o)
        def _():
            sum_buf[o + SPREAD, 0] += dk[:prompt_len]
            sum_buf[o + SPREAD, 1] += dv[:prompt_len]

    @pl.when(r == pl.num_programs(0) - 1)
    def _():
        own_ref[...] = sum_buf[SPREAD]
        for ref, o in zip(sent_refs, (-2, -1, 1, 2)):
            ref[...] = sum_buf[o + SPREAD].astype(BF16)


def backward_of(meta, pieces, blocks, per_step, scaled, probs, part, d_a, queries, keys, values, prompt_len,
                shard_rows, z_size):
    slots, query_len, width = queries.shape
    key_len = keys.shape[1]
    own_len = key_len - prompt_len
    heads = width // HEAD_SIZE
    cols = pieces[0].shape[1]
    depth_z = Y_SIZE * shard_rows
    by_slot = lambda *shape: pl.BlockSpec((1,) + shape, lambda r, m: (r, 0, 0))
    anywhere = pl.BlockSpec(memory_space=pl.ANY)
    whole = pl.BlockSpec((2, prompt_len, HEAD_SIZE), lambda r, m: (0, 0, 0))
    tile = lambda dtype: jax.ShapeDtypeStruct((2, prompt_len, HEAD_SIZE), dtype)
    return pl.pallas_call(
        functools.partial(backward_kernel, n_pieces=len(pieces), heads=heads, prompt_len=prompt_len, blocks=blocks,
                          per_step=per_step, shard_rows=shard_rows, z_size=z_size),
        grid_spec=pltpu.PrefetchScalarGridSpec(
            num_scalar_prefetch=1,
            grid=(slots,),
            in_specs=[anywhere] * (len(pieces) + 2) + [
                pl.BlockSpec((slots, query_len, cols), lambda r, m: (0, 0, 0)),
                by_slot(query_len, width - cols),
                by_slot(query_len, width),
                by_slot(key_len, HEAD_SIZE),
                by_slot(key_len, HEAD_SIZE),
            ],
            out_specs=[by_slot(query_len, width)] + [by_slot(own_len, HEAD_SIZE)] * 2 + [whole] * (2 * SPREAD + 1),
            scratch_shapes=load_scratch(slots, query_len, cols, len(blocks), per_step, depth_z) + [
                pltpu.VMEM((slots, key_len, heads * query_len), BF16),
                pltpu.VMEM((heads * query_len, HEAD_SIZE), BF16),
                pltpu.VMEM((heads * query_len, HEAD_SIZE), BF16),
                pltpu.VMEM((key_len, heads * query_len), BF16),
                pltpu.VMEM((2 * SPREAD + 1, 2, prompt_len, HEAD_SIZE), F32),
                pltpu.SemaphoreType.DMA((slots,)),
            ],
        ),
        out_shape=[jax.ShapeDtypeStruct((slots, query_len, width), BF16)]
        + [jax.ShapeDtypeStruct((slots, own_len, HEAD_SIZE), BF16)] * 2
        + [tile(F32)] + [tile(BF16)] * (2 * SPREAD),
        compiler_params=pltpu.CompilerParams(vmem_limit_bytes=VMEM_LIMIT),
        cost_estimate=pl.CostEstimate(
            flops=2 * slots * query_len * cols * depth_z * len(blocks) + 8 * slots * query_len * width * key_len,
            bytes_accessed=2 * depth_z * len(blocks) * (cols + slots * query_len),
            transcendentals=0,
        ),
    )(meta, *pieces, scaled, probs, part, d_a, queries, keys, values)


def after(values, *others):
    return lax.optimization_barrier((values, others))[0]


def on_device(queries, response_keys, response_values, out_grad, advantages, lengths, groups,
              prompt_keys, prompt_value_rows, w_out):
    slots, local_rows, width = out_grad.shape
    prompt_len = prompt_keys.shape[1]
    z_size = lax.axis_size("z")
    dp_count = z_size * lax.axis_size("y")
    my_z, my_y = lax.axis_index("z"), lax.axis_index("y")
    my_index = my_z * Y_SIZE + my_y
    tensor_index = lax.axis_index("x") * CORES + lax.axis_index("c")
    positions = tensor_index * local_rows + jnp.arange(local_rows, dtype=jnp.int32)
    live_mask = jnp.where(positions[None, :] < lengths[:, None], 1.0, 0.0).astype(F32)
    factor = advantages * live_mask * (loss_scale * RESPONSE_LENGTH / lengths.astype(F32))[:, None]
    scaled = (out_grad.astype(F32) * factor[:, :, None]).astype(BF16)
    half = w_out.shape[1] // 2
    w_a, w_b = w_out[:, :half], w_out[:, half:]
    shard_rows = w_out.shape[0]
    gathered = lax.all_gather(scaled, ("x", "c"), axis=1, tiled=True)
    z_parts = ring_gather(w_a, "z")
    b_inner = (0, -1, 1, 2)
    b_block = jnp.concatenate([w_b if dy == 0 else shift(w_b, "y", -dy) for dy in b_inner], 0)
    tile_pair = jnp.concatenate([prompt_keys[0], prompt_value_rows[0]], 0)
    tiles = {d: shift(tile_pair, ("z", "y"), -d) for d in (-2, -1, 1, 2)}
    a_block = jnp.concatenate([p[2] for p in z_parts], 0)
    a_block, tile_pair, tiles = lax.optimization_barrier((a_block, tile_pair, tiles))
    a_pieces = ring_gather(a_block, "y")

    raw_offsets = (groups - my_index) % dp_count
    offsets = jnp.where(raw_offsets > dp_count // 2, raw_offsets - dp_count, raw_offsets)
    tiles[0] = tile_pair

    meta = jnp.concatenate([jnp.stack([my_z, my_y]).astype(jnp.int32), offsets.astype(jnp.int32)])
    arrays = lambda pieces: [p[2] for p in pieces]

    received = jnp.zeros((slots,) + tile_pair.shape, BF16)
    for offset in range(-SPREAD, SPREAD + 1):
        received = jnp.where((offsets == offset)[:, None, None], tiles[offset][None], received)
    keys = jnp.concatenate([received[:, :prompt_len], response_keys], 1)
    values = jnp.concatenate([received[:, prompt_len:], response_values], 1)
    found = {"probs": probs_of(queries, keys, prompt_len)}

    def between(step, pieces, up, down):
        if step == 1:
            up, down, found["probs"] = lax.optimization_barrier((up, down, found["probs"]))
        elif step == 2:
            found["part"] = project(meta, arrays(pieces), blocks_of_b(pieces, b_inner, shard_rows), len(pieces),
                                    gathered, F32, shard_rows, z_size)
            up, down, found["part"] = lax.optimization_barrier((up, down, found["part"]))
        return up, down

    b_pieces = ring_gather(b_block, "z", between)
    order = [rel for rel, first, _ in z_parts if first == 0]
    late = b_pieces[3:]
    d_a = project(meta, arrays(a_pieces), blocks_of_a(a_pieces, order, shard_rows), 2, gathered, BF16, shard_rows, z_size)
    query_grad, key_grad, value_grad, own, *sent = backward_of(
        meta, arrays(late), blocks_of_b(late, b_inner, shard_rows), 1, gathered, found["probs"], found["part"], d_a,
        queries, keys, values, prompt_len, shard_rows, z_size)
    summed = own
    for offset, tile in zip((-2, -1, 1, 2), sent):
        summed = summed + shift(tile, ("z", "y"), offset).astype(F32)
    return query_grad, key_grad, value_grad, summed[:1], summed[1:]


def solution(mesh):
    dp_count, tensor_count = mesh.devices.shape
    fine = Mesh(
        mesh.devices.reshape(dp_count // Y_SIZE, Y_SIZE, tensor_count // CORES, CORES),
        ("z", "y", "x", "c"),
    )
    dp, tensor = ("z", "y"), ("x", "c")
    in_specs = (
        P(dp, None, tensor),
        P(dp, None, tensor),
        P(dp, None, tensor),
        P(dp, tensor, None),
        P(dp, tensor),
        P(dp),
        P(dp),
        P(dp, None, tensor),
        P(dp, None, tensor),
        P(dp, tensor),
    )
    out_specs = (P(dp, None, tensor),) * 5
    return jax.shard_map(on_device, mesh=fine, in_specs=in_specs, out_specs=out_specs, check_vma=False)
```
